128 devices in a mesh: subj: 4 (over x), fix: 32 (over z, y, core).
Axes of the slice: x: 4, y: 4, z: 4, core: 2. Of those that a mesh axis runs over, the one named last changes fastest.
Arguments:
- density: bfloat16 [1024, 65536], P(('subj', 'fix')), may hold values from -40 to 40, as said below
- conn_weight: bfloat16 [12288, 128, 128], P('fix'), may hold values from 9.983778e-07 to 1
- conn_rows: int32 [12288], P('fix'), may hold values from 0 to 16, as said below
- conn_cols: int32 [12288], P('fix'), may hold values from 0 to 47, as said below
- nbr_list: int32 [32, 32, 1], replicated, may hold values from 0 to 15
- design: int32 [1024, 64], P('subj'), may hold values from 0 to 15
Outputs:
- residual_scores: bfloat16 [1024, 65536], P('subj', 'fix')
- effect_scores: float32 [64, 65536], P(None, 'fix')
The draws below stay inside these ranges and needn't reach their ends.
Inputs may be any that keep to these rules, and one draw needn't show every extreme that they name: density's subject rows follow global subject order; values lie within the range. Each owner's filled slots, over all senders, have pairwise different (conn_rows, conn_cols) pairs; some owner has every slot from every sender filled, and every owner has an empty one unless all of its slots are filled. `conn_cols`: codes below 16 name the owner's own blocks, higher codes 16 + h + k the neighbour block taken from holder h; empty slots carry a code too.
All inputs are finite; a program needn't handle non-finite values.
Results may differ from the reference program's by a relative error of at most 0.0049.
Values may be sent and summed in bfloat16 or wider, within the bound.
A program may use at most 128 MiB of HBM per device.

```python
import math
import jax
import jax.numpy as jnp
from jax import lax

BLOCK = 128
COV = 64
FB_DEV = 16
NB_PEER = 1
CAP = 12
SOURCES = 48
SUBJECTS = 1024
FIXELS = 65536
N_FIX = 32


def draw_density(key, part):
    subkeys = jax.random.split(key, 3)
    rows_index = jnp.arange(SUBJECTS, dtype=jnp.float32)
    rising = 3.0 ** (rows_index / (SUBJECTS - 1))
    values = jax.random.normal(subkeys[0], (SUBJECTS, FIXELS), jnp.float32)
    jitter = jnp.exp(jax.random.uniform(subkeys[1], (SUBJECTS,), jnp.float32, -1.15, 1.15))
    column_scale = jnp.exp(jax.random.uniform(subkeys[2], (FIXELS,), jnp.float32, 0.0, 2.303))
    return jnp.clip(values * (rising * jitter)[:, None] * column_scale[None, :], -40.0, 40.0).astype(jnp.bfloat16)


def connection_layout(key):
    base_key = jax.random.fold_in(key, 11)
    subkeys = jax.random.split(base_key, 2)
    slot_total = N_FIX * CAP
    position_total = (FB_DEV + N_FIX * NB_PEER) * FB_DEV
    busy_total = max(1, N_FIX // 8)
    hot_owner = jax.random.permutation(subkeys[0], N_FIX) < busy_total

    def one_owner(owner_key, hot):
        split_keys = jax.random.split(owner_key, 3)
        shuffled = jax.random.permutation(split_keys[0], position_total)[:slot_total]
        shifted = (shuffled - shuffled[0] + position_total - 1) % position_total
        ranking = jax.random.permutation(split_keys[1], slot_total)
        filled_count = jax.random.randint(split_keys[2], (), slot_total // 8, slot_total // 2 + 1)
        filled = jnp.logical_or(hot, ranking < filled_count)
        row_codes = jnp.where(filled, shifted % FB_DEV, FB_DEV)
        col_codes = shifted // FB_DEV
        return (row_codes.astype(jnp.int32), col_codes.astype(jnp.int32))
    row_codes, col_codes = jax.vmap(one_owner)(jax.random.split(subkeys[1], N_FIX), hot_owner)
    row_codes = jnp.transpose(row_codes.reshape(N_FIX, N_FIX, CAP), (1, 0, 2)).reshape(-1)
    col_codes = jnp.transpose(col_codes.reshape(N_FIX, N_FIX, CAP), (1, 0, 2)).reshape(-1)
    return (row_codes, col_codes)


def draw_conn_rows(key, part):
    return connection_layout(key)[0]


def draw_conn_cols(key, part):
    return connection_layout(key)[1]


def with_ends(array, own_key, least, top_value):
    longest = array.shape.index(max(array.shape))
    spots = []
    for shift in (0, 1):
        where = [jax.random.randint(jax.random.fold_in(own_key, axis), (), 0, length) for axis, length in enumerate(array.shape)]
        where[longest] = (where[longest] + shift) % array.shape[longest]
        spots.append(tuple(where))
    return array.at[spots[0]].set(least).at[spots[1]].set(top_value)


def levels(key, dims, cuts, low, largest):
    loudness, own = 1.0, jax.random.fold_in(key, 6)
    for axis_at, shards_of in cuts:
        draws = jnp.exp(jax.random.uniform(jax.random.fold_in(own, axis_at), (shards_of,), jnp.float32, low / len(cuts), largest / len(cuts)))
        loudness = loudness * jnp.repeat(draws, dims[axis_at] // shards_of).reshape([-1 if axis == axis_at else 1 for axis in range(len(dims))])
    return loudness


def setup_inputs(seed: int = 0) -> dict:
    streams_of = jax.random.split(jax.random.key(seed), 7)
    return {
        "density": draw_density(jax.random.fold_in(streams_of[6], 71), 0),
        "conn_weight": jnp.clip(jnp.exp(math.log(1.0) - 13.817134 * jax.random.uniform(streams_of[1], (N_FIX * N_FIX * CAP, BLOCK, BLOCK), jnp.float32) ** levels(streams_of[1], (N_FIX * N_FIX * CAP, BLOCK, BLOCK), ((0, 32),), -0.2, 0.2)), 9.98377799987793e-07, 1.0).astype(jnp.bfloat16),
        "conn_rows": draw_conn_rows(jax.random.fold_in(streams_of[6], 71), 0),
        "conn_cols": draw_conn_cols(jax.random.fold_in(streams_of[6], 71), 0),
        "nbr_list": with_ends(jax.random.randint(streams_of[4], (N_FIX, N_FIX, NB_PEER), 0, FB_DEV), jax.random.fold_in(streams_of[4], 1), 0, FB_DEV - 1).astype(jnp.int32),
        "design": with_ends(jax.random.randint(streams_of[5], (SUBJECTS, COV), 0, 16), jax.random.fold_in(streams_of[5], 1), 0, 15).astype(jnp.int32),
    }


self_weight = 4.0
epsilon = 1e-06

def assemble(weights, row_codes, col_codes, blocks_dev, source_count):
    filled = row_codes < blocks_dev
    col_index = jnp.where(filled, col_codes, source_count).astype(jnp.int32)
    row_index = jnp.where(filled, row_codes, 0).astype(jnp.int32)
    block_size = weights.shape[-1]
    weight_table = jnp.zeros((source_count + 1, block_size, blocks_dev, block_size), weights.dtype)
    weight_table = weight_table.at[col_index, :, row_index, :].set(weights)
    return weight_table[:source_count].reshape(source_count * block_size, blocks_dev * block_size)

def solve_normal(gram, right_side):
    factor = jnp.linalg.cholesky(gram)
    first = lax.linalg.triangular_solve(factor, right_side, left_side=True, lower=True)
    coefficients = lax.linalg.triangular_solve(factor, first, left_side=True, lower=True, transpose_a=True)
    identity = jnp.eye(gram.shape[0], dtype=gram.dtype)
    partial_inverse = lax.linalg.triangular_solve(factor, identity, left_side=True, lower=True)
    inverse = lax.linalg.triangular_solve(factor, partial_inverse, left_side=True, lower=True, transpose_a=True)
    return (coefficients, jnp.diagonal(inverse))

def reference(density, conn_weight, conn_rows, conn_cols, nbr_list, design):
    density_blocks = density.reshape(SUBJECTS, N_FIX * FB_DEV, BLOCK)
    weight_grid = conn_weight.reshape(N_FIX, N_FIX, CAP, BLOCK, BLOCK)
    row_grid = conn_rows.reshape(N_FIX, N_FIX, CAP)
    col_grid = conn_cols.reshape(N_FIX, N_FIX, CAP)
    holders = jnp.arange(N_FIX, dtype=jnp.int32)

    def smooth_owner(owner_index):
        start_block = (owner_index * FB_DEV).astype(jnp.int32)
        own_blocks = lax.dynamic_slice_in_dim(density_blocks, start_block, FB_DEV, axis=1)
        chosen = lax.dynamic_index_in_dim(nbr_list, owner_index, 0, keepdims=False)
        block_ids = (holders[:, None] * FB_DEV + chosen).reshape(-1).astype(jnp.int32)
        neighbours = jnp.take(density_blocks, block_ids, axis=1)
        sources = jnp.concatenate([own_blocks, neighbours], axis=1)
        weights = lax.dynamic_index_in_dim(weight_grid, owner_index, 1, keepdims=False).reshape(N_FIX * CAP, BLOCK, BLOCK)
        row_codes = lax.dynamic_index_in_dim(row_grid, owner_index, 1, keepdims=False).reshape(-1)
        col_codes = lax.dynamic_index_in_dim(col_grid, owner_index, 1, keepdims=False).reshape(-1)
        weight_table = assemble(weights, row_codes, col_codes, FB_DEV, SOURCES)
        spread = jnp.dot(sources.reshape(SUBJECTS, SOURCES * BLOCK).astype(jnp.float32), weight_table.astype(jnp.float32), preferred_element_type=jnp.float32)
        own_wide = own_blocks.reshape(SUBJECTS, FB_DEV * BLOCK).astype(jnp.float32)
        return (self_weight * own_wide + spread).astype(jnp.bfloat16)
    stacked = lax.map(smooth_owner, holders)
    smoothed = jnp.transpose(stacked, (1, 0, 2)).reshape(SUBJECTS, FIXELS)
    covariates = (design.astype(jnp.float32) - 7.5) * 0.25
    cov_half = covariates.astype(jnp.bfloat16)
    gram = jnp.dot(cov_half.T.astype(jnp.float32), cov_half.astype(jnp.float32), preferred_element_type=jnp.float32)
    cross = jnp.dot(cov_half.T.astype(jnp.float32), smoothed.astype(jnp.float32), preferred_element_type=jnp.float32)
    coefficients, inverse_diag = solve_normal(gram, cross)
    residual = smoothed.astype(jnp.float32) - jnp.dot(covariates, coefficients, precision=lax.Precision.HIGHEST)
    variance = lax.optimization_barrier(jnp.sum(residual * residual, axis=0)) / (SUBJECTS - COV)
    scaling = lax.rsqrt(variance + epsilon)
    residual_scores = (residual * scaling[None, :]).astype(jnp.bfloat16)
    effect_scores = coefficients * scaling[None, :] * lax.rsqrt(inverse_diag)[:, None]
    return (residual_scores, effect_scores)
```

```python
import functools
import jax
import jax.numpy as jnp
from jax import lax
from jax.experimental import pallas as pl
from jax.experimental.pallas import tpu as pltpu
from jax.sharding import PartitionSpec as P

MESH = pl.DeviceIdType.MESH
SELF_WEIGHT = 4.0
EPSILON = 1e-06

NX, NF = 4, 32
BLOCK = 128
FB = 16
SRC = 48
CAP = 12
UNIT = 32
PER = BLOCK // UNIT
COV = 64
PEERS = NF - 1
PAIR = CAP * PER
QUART = 10
DIRECT = PAIR - 4 * QUART
NDIR = 2
LAG = 4
SLOTS = NF * CAP
COLS = FB * BLOCK
ROWS = 256
CHUNK = 2 * BLOCK
NCHUNK = COLS // CHUNK
GROUP = COLS // NX

_RING = ("01", "03", "10", "30", "11", "33", "13", "31", "20", "02", "12", "32", "21", "23", "22")
ORDER = [int(g[0]) * 8 + int(g[1]) * 2 + (c ^ (i & 1)) for c in (0, 1) for i, g in enumerate(_RING)] + [1]


def offset(k):
    words = [sum(v << (5 * i) for i, v in enumerate(ORDER[b : b + 6])) for b in range(0, PEERS, 6)]
    word = jnp.int32(words[0])
    for i in range(1, len(words)):
        word = jnp.where(k >= 6 * i, jnp.int32(words[i]), word)
    return (word >> (5 * lax.rem(k, 6))) & 31


def split(f):
    return f // 8, (f // 2) % 4, f % 2


def ahead(f, o):
    z, y, c = split(f)
    a, b, d = split(o)
    return lax.rem(z + a, 4) * 8 + lax.rem(y + b, 4) * 2 + lax.rem(c + d, 2)


def behind(f, o):
    z, y, c = split(f)
    a, b, d = split(o)
    return lax.rem(z + 4 - a, 4) * 8 + lax.rem(y + 4 - b, 4) * 2 + lax.rem(c + 2 - d, 2)


def remote(src, dst, send, recv, device):
    return pltpu.make_async_remote_copy(src, dst, send, recv, device_id=device, device_id_type=MESH)


def aligned(v, n):
    return pl.multiple_of(v, n)


def kernel(
    rows_ref, cols_ref, nbr_ref, dens_hbm, weight, design_t,
    scores, effects,
    dens, wbuf, stage, den, src, table, cstage, cbuf, idx_v, idx_s, gbuf, mat, linv, linvt, invd,
    smooth, resid, cov3, cpart, cin, bbuf, sqbuf,
    s_own, s_q, s_d, s_f, r_d, r_den, s_c, r_c, s_g, r_g, s_x, s_b, s_sq, r_sq,
    r_q, r_p, r_m, r_p2, r_m2, r_cin, r_b,
):
    x = lax.axis_index("subj")
    f = lax.axis_index("fix")
    xp, xm, x2 = lax.rem(x + 1, NX), lax.rem(x + 3, NX), lax.rem(x + 2, NX)
    half = QUART // 2
    dpart = DIRECT // NDIR

    own_dens = pltpu.make_async_copy(dens_hbm, dens, s_own.at[0])
    own_dens.start()
    own_rows = pl.ds(f * PAIR, PAIR)
    own_weight = pltpu.make_async_copy(weight.at[own_rows], wbuf.at[own_rows], s_own.at[1])
    own_weight.start()

    barrier = pltpu.get_barrier_semaphore()

    def greet(k, carry):
        pl.semaphore_signal(barrier, inc=1, device_id=(x, lax.rem(f + k, NF)), device_id_type=MESH)
        return carry

    lax.fori_loop(1, NF, greet, 0)
    for t in (xp, xm, x2):
        pl.semaphore_signal(barrier, inc=1, device_id=(t, f), device_id_type=MESH)
    pl.semaphore_wait(barrier, PEERS + 3)

    def send_quarter(i, carry):
        t = ahead(f, offset(i))
        remote(
            weight.at[pl.ds(t * PAIR + x * QUART, QUART)],
            wbuf.at[pl.ds(f * PAIR + x * QUART, QUART)],
            s_q, r_q.at[i], (x, t),
        ).start()
        return carry

    lax.fori_loop(0, PEERS, send_quarter, 0)

    cov_t = (design_t[...].astype(jnp.float32) - 7.5) * 0.25
    cov_wide = cov_t.T
    cov = cov_wide.astype(jnp.bfloat16)
    cov_half_t = cov_t.astype(jnp.bfloat16)
    for i in range(3):
        cov3[:, i * COV : (i + 1) * COV] = cov
    gbuf[x] = jnp.dot(cov_half_t, cov, preferred_element_type=jnp.float32)
    for t in (xp, xm, x2):
        remote(gbuf.at[x], gbuf.at[x], s_g, r_g, (t, f)).start()

    wbuf[SLOTS * PER :] = jnp.zeros((PER, UNIT, BLOCK), jnp.bfloat16)
    own_dens.wait()

    lane = lax.broadcasted_iota(jnp.int32, (8, BLOCK), 1)
    sub = lax.broadcasted_iota(jnp.int32, (8, BLOCK), 0)

    def gather_for(t):
        def own(c, carry):
            stage[t, c] = dens[t * FB + c]
            return carry

        def neighbour(h, carry):
            stage[t, FB + h] = dens[h * FB + nbr_ref[t, h]]
            return carry

        for c in range(FB):
            own(c, 0)
        for h in range(NF):
            neighbour(h, 0)
        codes = jnp.zeros((8, BLOCK), jnp.int32)
        for k in range(CAP):
            r = rows_ref[t * CAP + k]
            c = cols_ref[t * CAP + k]
            codes = jnp.where(lane == k, r * SRC + c, codes)
        cstage[t] = codes

    def send_side(i):
        t = ahead(f, offset(i))
        gather_for(t)
        remote(stage.at[t], den.at[f], s_d, r_den, (x, t)).start()
        remote(cstage.at[t], cbuf.at[f], s_c, r_c, (x, t)).start()

    def send_direct(i):
        t = ahead(f, offset(lax.rem(i, PEERS)))
        r = 4 * QUART + (i // PEERS) * dpart
        remote(
            weight.at[pl.ds(t * PAIR + r, dpart)],
            wbuf.at[pl.ds(f * PAIR + r, dpart)],
            s_d, r_d, (x, t),
        ).start()

    def pass_on(i):
        s = behind(f, offset(i))
        r = wbuf.at[pl.ds(s * PAIR + x * QUART, QUART)]
        remote(r, r, s_q, r_q.at[i], (x, f)).wait_recv()
        remote(r, r, s_f, r_p.at[i], (xp, f)).start()
        remote(r, r, s_f, r_m.at[i], (xm, f)).start()

    def pass_half(i):
        s = behind(f, offset(i))
        b = s * PAIR + xm * QUART
        r = wbuf.at[pl.ds(b, QUART)]
        remote(r, r, s_f, r_p.at[i], (xp, f)).wait_recv()
        r = wbuf.at[pl.ds(b, half)]
        remote(r, r, s_f, r_p2.at[i], (xp, f)).start()
        b = s * PAIR + xp * QUART
        r = wbuf.at[pl.ds(b, QUART)]
        remote(r, r, s_f, r_m.at[i], (xm, f)).wait_recv()
        r = wbuf.at[pl.ds(b + half, half)]
        remote(r, r, s_f, r_m2.at[i], (xm, f)).start()

    row_id = lax.broadcasted_iota(jnp.int32, (COV, 2 * COV), 0)
    lane_id = lax.broadcasted_iota(jnp.int32, (COV, 2 * COV), 1)

    def eliminate(j):
        m = mat[...]
        row = jnp.sum(jnp.where(row_id == j, m, 0.0), axis=0, keepdims=True)
        col = jnp.sum(jnp.where(lane_id == j, m, 0.0), axis=1, keepdims=True)
        pivot = jnp.sum(jnp.where((row_id == j) & (lane_id == j), m, 0.0), keepdims=True)
        factor = jnp.where(row_id > j, col / pivot, 0.0)
        mat[...] = m - factor * row

    def step(i, carry):
        @pl.when(i < PEERS)
        def _():
            pass_on(i)

        @pl.when(i >= LAG)
        def _():
            pass_half(i - LAG)

        @pl.when(i < PEERS)
        def _():
            send_side(i)
            for e in range(NDIR):
                send_direct(i * NDIR + e)

        return carry

    lax.fori_loop(0, PEERS + LAG, step, 0)

    whole = remote(gbuf.at[pl.ds(0, 3)], gbuf.at[pl.ds(0, 3)], s_g, r_g, (xp, f))
    whole.wait_recv()
    whole.wait_send()
    mat[:, :COV] = (gbuf[0] + gbuf[1]) + (gbuf[2] + gbuf[3])
    eye = (
        lax.broadcasted_iota(jnp.int32, (COV, COV), 0) == lax.broadcasted_iota(jnp.int32, (COV, COV), 1)
    )
    mat[:, COV:] = jnp.where(eye, 1.0, 0.0)

    def elim_step(j, carry):
        eliminate(j)
        return carry

    lax.fori_loop(0, COV, elim_step, 0)
    diag = jnp.sum(jnp.where(eye, mat[:, :COV], 0.0), axis=1, keepdims=True)
    lower = mat[:, COV:] / jnp.sqrt(diag)
    linv[...] = lower
    lower_t = lower.T
    linvt[...] = lower_t
    invd[...] = lax.rsqrt(jnp.sum(lower_t * lower_t, axis=1, keepdims=True))

    gather_for(f)
    den[f] = stage[f]
    cbuf[f] = cstage[f]
    rest = remote(cbuf.at[pl.ds(0, PEERS)], cbuf.at[pl.ds(0, PEERS)], s_c, r_c, (xp, f))
    rest.wait_recv()
    place = sub * BLOCK + lane

    def locate(s, acc):
        tile = cbuf[s]
        for k in range(CAP):
            acc = jnp.where(place == tile[:, k : k + 1], s * CAP + k, acc)
        return acc

    idx_v[...] = lax.fori_loop(0, NF, locate, jnp.full((8, BLOCK), SLOTS, jnp.int32))
    to_smem = pltpu.make_async_copy(idx_v, idx_s, s_own.at[0])
    to_smem.start()
    to_smem.wait()

    arrived = remote(den.at[pl.ds(0, PEERS)], den.at[pl.ds(0, PEERS)], s_d, r_den, (xp, f))
    arrived.wait_recv()

    def lay_out(c, carry):
        block = den[:, c].astype(jnp.float32).reshape(ROWS, BLOCK)
        src[:, pl.ds(aligned(c * BLOCK, BLOCK), BLOCK)] = block.astype(jnp.bfloat16)
        return carry

    lax.fori_loop(0, SRC, lay_out, 0)

    own_weight.wait()

    def last_halves(i, carry):
        r = wbuf.at[pl.ds(0, half)]
        remote(r, r, s_f, r_p2.at[i], (xp, f)).wait_recv()
        remote(r, r, s_f, r_m2.at[i], (xm, f)).wait_recv()
        return carry

    lax.fori_loop(0, PEERS, last_halves, 0)
    r = wbuf.at[pl.ds(0, PEERS * DIRECT)]
    remote(r, r, s_d, r_d, (xp, f)).wait_recv()

    def smooth_chunk(g):
        group = lax.rem(x + 1 + g // 2, NX)
        first = group * 4 + lax.rem(g, 2) * 2
        for c in range(SRC):
            for e in range(2):
                p = (first + e) * SRC + c
                i = idx_s[p // BLOCK, lax.rem(p, BLOCK)]
                for u in range(PER):
                    row = c * BLOCK + u * UNIT
                    table[row : row + UNIT, e * BLOCK : (e + 1) * BLOCK] = wbuf[i * PER + u]
        spread = jnp.dot(src[...], table[...], preferred_element_type=jnp.float32)
        at = pl.ds(aligned(first * BLOCK, BLOCK), CHUNK)
        part = (SELF_WEIGHT * src[:, at].astype(jnp.float32) + spread).astype(jnp.bfloat16)
        smooth[:, at] = part
        cpart[g] = jnp.dot(cov_half_t, part, preferred_element_type=jnp.float32)

    def send_chunk(g, carry):
        smooth_chunk(g)
        rel = g // 2
        remote(
            cpart.at[g], cin.at[rel, lax.rem(g, 2)], s_x, r_cin.at[g], (lax.rem(x + 1 + rel, NX), f)
        ).start()
        return carry

    lax.fori_loop(0, NCHUNK - 2, send_chunk, 0)

    def keep_chunk(g, carry):
        smooth_chunk(g)
        return carry

    lax.fori_loop(NCHUNK - 2, NCHUNK, keep_chunk, 0)

    for h in range(2):
        total = cpart[NCHUNK - 2 + h]
        for rel in range(3):
            remote(cpart.at[0], cin.at[rel, h], s_x, r_cin.at[rel * 2 + h], (xp, f)).wait_recv()
            total = total + cin[rel, h]
        y = jnp.dot(linv[...], total, preferred_element_type=jnp.float32, precision=lax.Precision.HIGHEST)
        bbuf[x, :, h * CHUNK : (h + 1) * CHUNK] = jnp.dot(
            linvt[...], y, preferred_element_type=jnp.float32, precision=lax.Precision.HIGHEST
        )
    for rel, t in enumerate((xp, x2, xm)):
        remote(bbuf.at[x], bbuf.at[x], s_b, r_b.at[rel], (t, f)).start()

    def residual(group):
        at = pl.ds(aligned(group * GROUP, GROUP), GROUP)
        beta = bbuf[group]
        b1 = beta.astype(jnp.bfloat16)
        left = beta - b1.astype(jnp.float32)
        b2 = left.astype(jnp.bfloat16)
        b3 = (left - b2.astype(jnp.float32)).astype(jnp.bfloat16)
        parts = jnp.concatenate([b1, b2, b3], axis=0)
        fitted = jnp.dot(cov3[...], parts, preferred_element_type=jnp.float32)
        res = smooth[:, at].astype(jnp.float32) - fitted
        resid[:, at] = res
        sqbuf[x, :, at] = jnp.sum(res * res, axis=0, keepdims=True)

    residual(x)
    for rel, t in enumerate((xm, x2, xp)):
        remote(bbuf.at[t], bbuf.at[t], s_b, r_b.at[rel], (t, f)).wait_recv()
        residual(t)
    for t in (xp, xm, x2):
        remote(sqbuf.at[x], sqbuf.at[x], s_sq, r_sq, (t, f)).start()
    whole = remote(sqbuf.at[pl.ds(0, 3)], sqbuf.at[pl.ds(0, 3)], s_sq, r_sq, (xp, f))
    whole.wait_recv()
    variance = ((sqbuf[0] + sqbuf[1]) + (sqbuf[2] + sqbuf[3])) / (ROWS * NX - COV)
    scaling = lax.rsqrt(variance + EPSILON)
    scores[...] = (resid[...] * scaling).astype(jnp.bfloat16)
    for g in range(NX):
        at = slice(g * GROUP, (g + 1) * GROUP)
        effects[:, at] = bbuf[g] * scaling[:, at] * invd[...]

    r = wbuf.at[pl.ds(0, PEERS * QUART)]
    remote(r, r, s_q, r_d, (xp, f)).wait_send()
    r = wbuf.at[pl.ds(0, 3 * PEERS * QUART)]
    remote(r, r, s_f, r_d, (xp, f)).wait_send()
    r = wbuf.at[pl.ds(0, PEERS * (DIRECT + SRC * 8 // UNIT))]
    remote(r, r, s_d, r_d, (xp, f)).wait_send()
    rest.wait_send()
    r = cpart.at[pl.ds(0, NCHUNK - 2)]
    remote(r, r, s_x, r_d, (xp, f)).wait_send()
    r = bbuf.at[pl.ds(0, 3)]
    remote(r, r, s_b, r_d, (xp, f)).wait_send()
    whole.wait_send()


def shards(density, conn_weight, conn_rows, conn_cols, nbr_list, design):
    dens = density.reshape(8, NF * FB, BLOCK).transpose(1, 0, 2)
    weight = conn_weight.reshape(NF * PAIR, UNIT, BLOCK)
    smem = pl.BlockSpec(memory_space=pltpu.SMEM)
    anywhere = pl.BlockSpec(memory_space=pl.ANY)
    vmem = pl.BlockSpec(memory_space=pltpu.VMEM)
    f32, bf16, i32 = jnp.float32, jnp.bfloat16, jnp.int32
    dma = pltpu.SemaphoreType.DMA
    return pl.pallas_call(
        kernel,
        out_shape=(
            jax.ShapeDtypeStruct((ROWS, COLS), bf16),
            jax.ShapeDtypeStruct((COV, COLS), f32),
        ),
        in_specs=[smem, smem, smem, anywhere, anywhere, vmem],
        out_specs=(vmem, vmem),
        scratch_shapes=[
            pltpu.VMEM((NF * FB, 8, BLOCK), bf16),
            pltpu.VMEM(((SLOTS + 1) * PER, UNIT, BLOCK), bf16),
            pltpu.VMEM((NF, SRC, 8, BLOCK), bf16),
            pltpu.VMEM((NF, SRC, 8, BLOCK), bf16),
            pltpu.VMEM((ROWS, SRC * BLOCK), bf16),
            pltpu.VMEM((SRC * BLOCK, CHUNK), bf16),
            pltpu.VMEM((NF, 8, BLOCK), i32),
            pltpu.VMEM((NF, 8, BLOCK), i32),
            pltpu.VMEM((8, BLOCK), i32),
            pltpu.SMEM((8, BLOCK), i32),
            pltpu.VMEM((NX, COV, COV), f32),
            pltpu.VMEM((COV, 2 * COV), f32),
            pltpu.VMEM((COV, COV), f32),
            pltpu.VMEM((COV, COV), f32),
            pltpu.VMEM((COV, 1), f32),
            pltpu.VMEM((ROWS, COLS), bf16),
            pltpu.VMEM((ROWS, COLS), f32),
            pltpu.VMEM((ROWS, 3 * COV), bf16),
            pltpu.VMEM((NCHUNK, COV, CHUNK), f32),
            pltpu.VMEM((3, 2, COV, CHUNK), f32),
            pltpu.VMEM((NX, COV, GROUP), f32),
            pltpu.VMEM((NX, 1, COLS), f32),
            dma((2,)),
        ]
        + [dma] * 13
        + [dma((PEERS,))] * 5
        + [dma((NCHUNK - 2,)), dma((3,))],
        compiler_params=pltpu.CompilerParams(
            collective_id=0, has_side_effects=True, vmem_limit_bytes=60 * 2**20
        ),
        cost_estimate=pl.CostEstimate(flops=2 * ROWS * SRC * BLOCK * COLS, bytes_accessed=30 << 20, transcendentals=0),
    )(conn_rows, conn_cols, nbr_list.reshape(NF, NF), dens, weight, design.T)


def solution(mesh):
    in_specs = (
        P(("subj", "fix"), None),
        P("fix", None, None),
        P("fix"),
        P("fix"),
        P(),
        P("subj", None),
    )
    out_specs = (P("subj", "fix"), P(None, "fix"))
    return jax.shard_map(shards, mesh=mesh, in_specs=in_specs, out_specs=out_specs, check_vma=False)
```

```python
import functools
import jax
import jax.numpy as jnp
from jax import lax
from jax.experimental import pallas as pl
from jax.experimental.pallas import tpu as pltpu
from jax.sharding import PartitionSpec as P

MESH = pl.DeviceIdType.MESH
SELF_WEIGHT = 4.0
EPSILON = 1e-06

NX, NF = 4, 32
BLOCK = 128
FB = 16
SRC = 48
CAP = 12
UNIT = 32
PER = BLOCK // UNIT
COV = 64
PEERS = NF - 2
PAIR = CAP * PER
QUART = 10
DIRECT = PAIR - 4 * QUART
NDIR = 2
LAG = 4
ELIM_AT = 4
LAY_AT = 28
LAY_STEP = 8
KSTEP = 8
SLOTS = NF * CAP
COLS = FB * BLOCK
ROWS = 256
CHUNK = 2 * BLOCK
NCHUNK = COLS // CHUNK
GROUP = COLS // NX

_RING = ("01", "03", "10", "30", "11", "33", "13", "31", "20", "02", "12", "32", "21", "23", "22")
ORDER = [int(g[0]) * 8 + int(g[1]) * 2 + (c ^ (i & 1)) for c in (0, 1) for i, g in enumerate(_RING)]


def offset(k):
    words = [sum(v << (5 * i) for i, v in enumerate(ORDER[b : b + 6])) for b in range(0, PEERS, 6)]
    word = jnp.int32(words[0])
    for i in range(1, len(words)):
        word = jnp.where(k >= 6 * i, jnp.int32(words[i]), word)
    return (word >> (5 * lax.rem(k, 6))) & 31


def split(f):
    return f // 8, (f // 2) % 4, f % 2


def ahead(f, o):
    z, y, c = split(f)
    a, b, d = split(o)
    turn = 1 - 2 * c
    return lax.rem(z + 4 + turn * a, 4) * 8 + lax.rem(y + 4 + turn * b, 4) * 2 + lax.rem(c + d, 2)


def behind(f, o):
    z, y, c = split(f)
    a, b, d = split(o)
    sender = lax.rem(c + d, 2)
    turn = 1 - 2 * sender
    return lax.rem(z + 4 - turn * a, 4) * 8 + lax.rem(y + 4 - turn * b, 4) * 2 + sender


def remote(src, dst, send, recv, device):
    return pltpu.make_async_remote_copy(src, dst, send, recv, device_id=device, device_id_type=MESH)


def three(v):
    a = v.astype(jnp.bfloat16)
    v = v - a.astype(jnp.float32)
    b = v.astype(jnp.bfloat16)
    return a, b, (v - b.astype(jnp.float32)).astype(jnp.bfloat16)


def aligned(v, n):
    return pl.multiple_of(v, n)


def kernel(
    rows_ref, cols_ref, nbr_ref, dens_hbm, weight, design_t,
    resid_hbm, coef_hbm, scaling,
    dens, wbuf, stage, den, src, cstage, cbuf, idx_v, idx_s, gbuf, mat, solver, invd,
    smooth, resid, coef, cov3, cpart, cin, bbuf, sqbuf,
    s_own, s_q, s_d, s_f, r_d, r_den, s_g, r_g, s_x, s_b, s_sq, r_sq, s_out, s_sib, s_c, r_c,
    r_q, r_p, r_m, r_p2, r_m2, r_cin, r_b,
):
    x = lax.axis_index("subj")
    f = lax.axis_index("fix")
    xp, xm, x2 = lax.rem(x + 1, NX), lax.rem(x + 3, NX), lax.rem(x + 2, NX)
    half = QUART // 2
    dpart = DIRECT // NDIR

    own_dens = pltpu.make_async_copy(dens_hbm, dens, s_own.at[0])
    own_dens.start()
    own_rows = pl.ds(f * PAIR, PAIR)
    own_weight = pltpu.make_async_copy(weight.at[own_rows], wbuf.at[own_rows], s_own.at[1])
    own_weight.start()

    barrier = pltpu.get_barrier_semaphore()

    def greet(k, carry):
        pl.semaphore_signal(barrier, inc=1, device_id=(x, lax.rem(f + k, NF)), device_id_type=MESH)
        return carry

    lax.fori_loop(1, NF, greet, 0)
    for t in (xp, xm, x2):
        pl.semaphore_signal(barrier, inc=1, device_id=(t, f), device_id_type=MESH)
    pl.semaphore_wait(barrier, NF - 1 + 3)

    def send_quarter(i, carry):
        t = ahead(f, offset(i))
        remote(
            weight.at[pl.ds(t * PAIR + x * QUART, QUART)],
            wbuf.at[pl.ds(f * PAIR + x * QUART, QUART)],
            s_q, r_q.at[i], (x, t),
        ).start()
        return carry

    lax.fori_loop(0, PEERS, send_quarter, 0)

    sib = f + 1 - 2 * lax.rem(f, 2)

    def to_sibling():
        return remote(
            weight.at[pl.ds(sib * PAIR, PAIR)], wbuf.at[pl.ds(f * PAIR, PAIR)], s_sib.at[0], s_sib.at[1], (x, sib)
        )

    to_sibling().start()

    cov_t = (design_t[...].astype(jnp.float32) - 7.5) * 0.25
    cov_wide = cov_t.T
    cov = cov_wide.astype(jnp.bfloat16)
    cov_half_t = cov_t.astype(jnp.bfloat16)
    for i in range(3):
        cov3[:, i * COV : (i + 1) * COV] = cov
    gbuf[x] = jnp.dot(cov_half_t, cov, preferred_element_type=jnp.float32)
    for t in (xp, xm, x2):
        remote(gbuf.at[x], gbuf.at[x], s_g, r_g, (t, f)).start()

    wbuf[SLOTS * PER :] = jnp.zeros((PER, UNIT, BLOCK), jnp.bfloat16)
    own_dens.wait()

    lane = lax.broadcasted_iota(jnp.int32, (8, BLOCK), 1)
    sub = lax.broadcasted_iota(jnp.int32, (8, BLOCK), 0)

    def gather_for(t):
        def own(c, carry):
            stage[t, c] = dens[t * FB + c]
            return carry

        def neighbour(h, carry):
            stage[t, FB + h] = dens[h * FB + nbr_ref[t, h]]
            return carry

        for c in range(FB):
            own(c, 0)
        for h in range(NF):
            neighbour(h, 0)
    spot = sub * BLOCK + lane

    def codes_for(t):
        codes = jnp.zeros((1, BLOCK), jnp.int32)
        for k in range(CAP):
            code = rows_ref[t * CAP + k] * SRC + cols_ref[t * CAP + k]
            codes = jnp.where(lane[:1] == k, code, codes)
        return codes

    def send_side(t):
        gather_for(t)
        cstage[t] = codes_for(t)
        remote(cstage.at[t], cbuf.at[f], s_c, r_c, (x, t)).start()
        remote(stage.at[t], den.at[f], s_d, r_den, (x, t)).start()

    def send_direct(i):
        t = ahead(f, offset(lax.rem(i, PEERS)))
        r = 4 * QUART + (i // PEERS) * dpart
        remote(
            weight.at[pl.ds(t * PAIR + r, dpart)],
            wbuf.at[pl.ds(f * PAIR + r, dpart)],
            s_d, r_d, (x, t),
        ).start()

    def pass_on(i):
        s = behind(f, offset(i))
        r = wbuf.at[pl.ds(s * PAIR + x * QUART, QUART)]
        remote(r, r, s_q, r_q.at[i], (x, f)).wait_recv()
        remote(r, r, s_f, r_p.at[i], (xp, f)).start()
        remote(r, r, s_f, r_m.at[i], (xm, f)).start()

    def pass_half(i):
        s = behind(f, offset(i))
        b = s * PAIR + xm * QUART
        r = wbuf.at[pl.ds(b, QUART)]
        remote(r, r, s_f, r_p.at[i], (xp, f)).wait_recv()
        r = wbuf.at[pl.ds(b, half)]
        remote(r, r, s_f, r_p2.at[i], (xp, f)).start()
        b = s * PAIR + xp * QUART
        r = wbuf.at[pl.ds(b, QUART)]
        remote(r, r, s_f, r_m.at[i], (xm, f)).wait_recv()
        r = wbuf.at[pl.ds(b + half, half)]
        remote(r, r, s_f, r_m2.at[i], (xm, f)).start()

    row_id = lax.broadcasted_iota(jnp.int32, (COV, 2 * COV), 0)
    lane_id = lax.broadcasted_iota(jnp.int32, (COV, 2 * COV), 1)

    def eliminate(j):
        m = mat[...]
        row = jnp.sum(jnp.where(row_id == j, m, 0.0), axis=0, keepdims=True)
        col = jnp.sum(jnp.where(lane_id == j, m, 0.0), axis=1, keepdims=True)
        pivot = jnp.sum(jnp.where((row_id == j) & (lane_id == j), m, 0.0), keepdims=True)
        factor = jnp.where(row_id > j, col / pivot, 0.0)
        mat[...] = m - factor * row

    eye = (
        lax.broadcasted_iota(jnp.int32, (COV, COV), 0) == lax.broadcasted_iota(jnp.int32, (COV, COV), 1)
    )

    def all_gram():
        return remote(gbuf.at[pl.ds(0, 3)], gbuf.at[pl.ds(0, 3)], s_g, r_g, (xp, f))

    def all_codes():
        return remote(cbuf.at[pl.ds(0, NF - 1)], cbuf.at[pl.ds(0, NF - 1)], s_c, r_c, (xp, f))

    def locate(s, acc):
        tile = cbuf[s]
        for k in range(CAP):
            acc = jnp.where(spot == tile[:, k : k + 1], s * CAP + k, acc)
        return acc

    def lay_out(c):
        block = den[:, c].astype(jnp.float32).reshape(ROWS, BLOCK)
        src[:, pl.ds(aligned(c * BLOCK, BLOCK), BLOCK)] = block.astype(jnp.bfloat16)

    def step(i, carry):
        @pl.when(i < PEERS)
        def _():
            pass_on(i)

        @pl.when(i >= LAG)
        def _():
            pass_half(i - LAG)

        @pl.when(i < PEERS // 2)
        def _():
            for e in range(2):
                send_side(ahead(f, offset(2 * i + e)))

        @pl.when((i >= PEERS // 2) & (i < PEERS))
        def _():
            for e in range(2 * NDIR):
                send_direct((i - PEERS // 2) * 2 * NDIR + e)

        @pl.when(i == ELIM_AT - 1)
        def _():
            all_gram().wait_recv()
            mat[:, :COV] = (gbuf[0] + gbuf[1]) + (gbuf[2] + gbuf[3])
            mat[:, COV:] = jnp.where(eye, 1.0, 0.0)

        @pl.when((i >= ELIM_AT) & (i < ELIM_AT + COV // 4))
        def _():
            for e in range(4):
                eliminate((i - ELIM_AT) * 4 + e)

        @pl.when(i == ELIM_AT + COV // 4)
        def _():
            diag = jnp.sum(jnp.where(eye, mat[:, :COV], 0.0), axis=1, keepdims=True)
            lower = mat[:, COV:] / jnp.sqrt(diag)
            lower_t = lower.T
            inverse = jnp.dot(lower_t, lower, preferred_element_type=jnp.float32, precision=lax.Precision.HIGHEST)
            g1, g2, g3 = three(inverse)
            solver[...] = jnp.concatenate([g1, g1, g1, g2, g2, g3], axis=1)
            invd[...] = lax.rsqrt(jnp.sum(lower_t * lower_t, axis=1, keepdims=True))

        @pl.when(i == LAY_AT - 1)
        def _():
            all_codes().wait_recv()
            idx_v[...] = lax.fori_loop(0, NF, locate, jnp.full((8, BLOCK), SLOTS, jnp.int32))
            to_smem = pltpu.make_async_copy(idx_v, idx_s, s_own.at[0])
            to_smem.start()
            to_smem.wait()

        @pl.when(i == LAY_AT - 1)
        def _():
            remote(den.at[pl.ds(0, NF - 1)], den.at[pl.ds(0, NF - 1)], s_d, r_den, (xp, f)).wait_recv()

        for e in range(LAY_STEP):
            c = (i - LAY_AT) * LAY_STEP + e

            @pl.when((c >= 0) & (c < SRC))
            def _():
                lay_out(c)

        return carry

    send_side(sib)
    gather_for(f)
    den[f] = stage[f]
    cbuf[f] = codes_for(f)
    lax.fori_loop(0, PEERS + LAG, step, 0)

    own_weight.wait()
    to_sibling().wait_recv()

    def last_halves(i, carry):
        r = wbuf.at[pl.ds(0, half)]
        remote(r, r, s_f, r_p2.at[i], (xp, f)).wait_recv()
        remote(r, r, s_f, r_m2.at[i], (xm, f)).wait_recv()
        return carry

    lax.fori_loop(0, PEERS, last_halves, 0)
    r = wbuf.at[pl.ds(0, PEERS * DIRECT)]
    remote(r, r, s_d, r_d, (xp, f)).wait_recv()

    def smooth_pair(n, halves):
        firsts = [group * 4 + h * 2 for group, h in halves]

        def block(first, c):
            p = first * SRC + c
            i = idx_s[p // BLOCK, lax.rem(p, BLOCK)]
            return jnp.concatenate([wbuf[i * PER + u] for u in range(PER)], axis=0)

        spread = None
        for c0 in range(0, SRC, KSTEP):
            right = jnp.concatenate(
                [
                    jnp.concatenate([block(first + e, c) for first in firsts for e in range(2)], axis=1)
                    for c in range(c0, c0 + KSTEP)
                ],
                axis=0,
            )
            part = jnp.dot(
                src[:, c0 * BLOCK : (c0 + KSTEP) * BLOCK], right, preferred_element_type=jnp.float32
            )
            spread = part if spread is None else spread + part
        for e, first in enumerate(firsts):
            at = pl.ds(aligned(first * BLOCK, BLOCK), CHUNK)
            own = src[:, at].astype(jnp.float32)
            part = (SELF_WEIGHT * own + spread[:, e * CHUNK : (e + 1) * CHUNK]).astype(jnp.bfloat16)
            smooth[:, at] = part
            cpart[2 * n + e] = jnp.dot(cov_half_t, part, preferred_element_type=jnp.float32)

    def send_part(n, rel, h, t):
        remote(cpart.at[n], cin.at[rel, h], s_x, r_cin.at[rel * 2 + h], (t, f)).start()

    smooth_pair(0, ((x2, 0), (x2, 1)))
    send_part(0, 0, 0, x2)
    send_part(1, 0, 1, x2)
    for h in range(2):
        smooth_pair(1 + h, ((xp, h), (xm, h)))
        send_part(2 + 2 * h, 1, h, xp)
        send_part(3 + 2 * h, 2, h, xm)
    smooth_pair(3, ((x, 0), (x, 1)))

    for h in range(2):
        total = cpart[NCHUNK - 2 + h]
        for rel in range(3):
            remote(cpart.at[0], cin.at[rel, h], s_x, r_cin.at[rel * 2 + h], (xp, f)).wait_recv()
            total = total + cin[rel, h]
        t1, t2, t3 = three(total)
        right = jnp.concatenate([t1, t2, t3, t1, t2, t1], axis=0)
        bbuf[x, :, h * CHUNK : (h + 1) * CHUNK] = jnp.dot(solver[...], right, preferred_element_type=jnp.float32)
    for rel, t in enumerate((xp, xm, x2)):
        remote(bbuf.at[x], bbuf.at[x], s_b, r_b.at[rel], (t, f)).start()

    def residual(group):
        at = pl.ds(aligned(group * GROUP, GROUP), GROUP)
        beta = bbuf[group]
        parts = jnp.concatenate(three(beta), axis=0)
        fitted = jnp.dot(cov3[...], parts, preferred_element_type=jnp.float32)
        res = smooth[:, at].astype(jnp.float32) - fitted
        resid[group] = res
        pltpu.make_async_copy(resid.at[group], resid_hbm.at[:, at], s_out).start()
        sqbuf[x, :, at] = jnp.sum(res * res, axis=0, keepdims=True)

    residual(x)
    for rel, t in enumerate((xm, xp, x2)):
        remote(bbuf.at[t], bbuf.at[t], s_b, r_b.at[rel], (t, f)).wait_recv()
        residual(t)
    for t in (xp, xm, x2):
        remote(sqbuf.at[x], sqbuf.at[x], s_sq, r_sq, (t, f)).start()
    for g in range(NX):
        coef[:, g * GROUP : (g + 1) * GROUP] = bbuf[g] * invd[...]
    pltpu.make_async_copy(coef, coef_hbm, s_own.at[1]).start()
    whole = remote(sqbuf.at[pl.ds(0, 3)], sqbuf.at[pl.ds(0, 3)], s_sq, r_sq, (xp, f))
    whole.wait_recv()
    variance = ((sqbuf[0] + sqbuf[1]) + (sqbuf[2] + sqbuf[3])) / (ROWS * NX - COV)
    scaling[...] = lax.rsqrt(variance + EPSILON)

    pltpu.make_async_copy(resid, resid, s_out).wait()
    pltpu.make_async_copy(coef, coef_hbm, s_own.at[1]).wait()
    r = wbuf.at[pl.ds(0, PEERS * QUART)]
    remote(r, r, s_q, r_d, (xp, f)).wait_send()
    r = wbuf.at[pl.ds(0, 3 * PEERS * QUART)]
    remote(r, r, s_f, r_d, (xp, f)).wait_send()
    r = wbuf.at[pl.ds(0, PEERS * DIRECT + (NF - 1) * SRC * 8 // UNIT)]
    remote(r, r, s_d, r_d, (xp, f)).wait_send()
    to_sibling().wait_send()
    all_gram().wait_send()
    all_codes().wait_send()
    r = cpart.at[pl.ds(0, NCHUNK - 2)]
    remote(r, r, s_x, r_d, (xp, f)).wait_send()
    r = bbuf.at[pl.ds(0, 3)]
    remote(r, r, s_b, r_d, (xp, f)).wait_send()
    whole.wait_send()


def shards(density, conn_weight, conn_rows, conn_cols, nbr_list, design):
    dens = density.reshape(8, NF * FB, BLOCK).transpose(1, 0, 2)
    weight = conn_weight.reshape(NF * PAIR, UNIT, BLOCK)
    smem = pl.BlockSpec(memory_space=pltpu.SMEM)
    anywhere = pl.BlockSpec(memory_space=pl.ANY)
    vmem = pl.BlockSpec(memory_space=pltpu.VMEM)
    f32, bf16, i32 = jnp.float32, jnp.bfloat16, jnp.int32
    dma = pltpu.SemaphoreType.DMA
    residual, coefficients, scaling = pl.pallas_call(
        kernel,
        out_shape=(
            jax.ShapeDtypeStruct((ROWS, COLS), f32),
            jax.ShapeDtypeStruct((COV, COLS), f32),
            jax.ShapeDtypeStruct((1, COLS), f32),
        ),
        in_specs=[smem, smem, smem, anywhere, anywhere, vmem],
        out_specs=(anywhere, anywhere, vmem),
        scratch_shapes=[
            pltpu.VMEM((NF * FB, 8, BLOCK), bf16),
            pltpu.VMEM(((SLOTS + 1) * PER, UNIT, BLOCK), bf16),
            pltpu.VMEM((NF, SRC, 8, BLOCK), bf16),
            pltpu.VMEM((NF, SRC, 8, BLOCK), bf16),
            pltpu.VMEM((ROWS, SRC * BLOCK), bf16),
            pltpu.VMEM((NF, 1, BLOCK), i32),
            pltpu.VMEM((NF, 1, BLOCK), i32),
            pltpu.VMEM((8, BLOCK), i32),
            pltpu.SMEM((8, BLOCK), i32),
            pltpu.VMEM((NX, COV, COV), f32),
            pltpu.VMEM((COV, 2 * COV), f32),
            pltpu.VMEM((COV, 6 * COV), bf16),
            pltpu.VMEM((COV, 1), f32),
            pltpu.VMEM((ROWS, COLS), bf16),
            pltpu.VMEM((NX, ROWS, GROUP), f32),
            pltpu.VMEM((COV, COLS), f32),
            pltpu.VMEM((ROWS, 3 * COV), bf16),
            pltpu.VMEM((NCHUNK, COV, CHUNK), f32),
            pltpu.VMEM((3, 2, COV, CHUNK), f32),
            pltpu.VMEM((NX, COV, GROUP), f32),
            pltpu.VMEM((NX, 1, COLS), f32),
            dma((2,)),
        ]
        + [dma] * 12
        + [dma((2,)), dma, dma]
        + [dma((PEERS,))] * 5
        + [dma((NCHUNK - 2,)), dma((3,))],
        compiler_params=pltpu.CompilerParams(
            collective_id=0, has_side_effects=True, vmem_limit_bytes=60 * 2**20
        ),
        cost_estimate=pl.CostEstimate(flops=2 * ROWS * SRC * BLOCK * COLS, bytes_accessed=30 << 20, transcendentals=0),
    )(conn_rows, conn_cols, nbr_list.reshape(NF, NF), dens, weight, design.T)
    return (residual * scaling).astype(bf16), coefficients * scaling


def solution(mesh):
    in_specs = (
        P(("subj", "fix"), None),
        P("fix", None, None),
        P("fix"),
        P("fix"),
        P(),
        P("subj", None),
    )
    out_specs = (P("subj", "fix"), P(None, "fix"))
    return jax.shard_map(shards, mesh=mesh, in_specs=in_specs, out_specs=out_specs, check_vma=False)
```

```python
import functools
import jax
import jax.numpy as jnp
from jax import lax
from jax.experimental import pallas as pl
from jax.experimental.pallas import tpu as pltpu
from jax.sharding import PartitionSpec as P

MESH = pl.DeviceIdType.MESH
SELF_WEIGHT = 4.0
EPSILON = 1e-06

NX, NF = 4, 32
BLOCK = 128
FB = 16
SRC = 48
CAP = 12
UNIT = 32
PER = BLOCK // UNIT
COV = 64
PEERS = NF - 2
PAIR = CAP * PER
QUART = 10
DIRECT = PAIR - 4 * QUART
NDIR = 2
LAG = 4
ELIM_AT = 4
LAY_AT = 28
LAY_STEP = 8
KSTEP = 8
SLOTS = NF * CAP
COLS = FB * BLOCK
ROWS = 256
CHUNK = 2 * BLOCK
NCHUNK = COLS // CHUNK
GROUP = COLS // NX

_RING = ("01", "03", "10", "30", "11", "33", "13", "31", "20", "02", "12", "32", "21", "23", "22")
ORDER = [int(g[0]) * 8 + int(g[1]) * 2 + (c ^ (i & 1)) for c in (0, 1) for i, g in enumerate(_RING)]


def offset(k):
    words = [sum(v << (5 * i) for i, v in enumerate(ORDER[b : b + 6])) for b in range(0, PEERS, 6)]
    word = jnp.int32(words[0])
    for i in range(1, len(words)):
        word = jnp.where(k >= 6 * i, jnp.int32(words[i]), word)
    return (word >> (5 * lax.rem(k, 6))) & 31


def split(f):
    return f // 8, (f // 2) % 4, f % 2


def ahead(f, o):
    z, y, c = split(f)
    a, b, d = split(o)
    turn = 1 - 2 * c
    return lax.rem(z + 4 + turn * a, 4) * 8 + lax.rem(y + 4 + turn * b, 4) * 2 + lax.rem(c + d, 2)


def behind(f, o):
    z, y, c = split(f)
    a, b, d = split(o)
    sender = lax.rem(c + d, 2)
    turn = 1 - 2 * sender
    return lax.rem(z + 4 - turn * a, 4) * 8 + lax.rem(y + 4 - turn * b, 4) * 2 + sender


def remote(src, dst, send, recv, device):
    return pltpu.make_async_remote_copy(src, dst, send, recv, device_id=device, device_id_type=MESH)


def three(v):
    a = v.astype(jnp.bfloat16)
    v = v - a.astype(jnp.float32)
    b = v.astype(jnp.bfloat16)
    return a, b, (v - b.astype(jnp.float32)).astype(jnp.bfloat16)


def aligned(v, n):
    return pl.multiple_of(v, n)


def kernel(
    rows_ref, cols_ref, nbr_ref, dens_hbm, weight, design_t,
    resid, coef, scaling,
    dens, wbuf, stage, den, src, cstage, cbuf, idx_v, idx_s, gbuf, mat, solver, invd,
    smooth, cov3, cpart, cin, bbuf, sqbuf,
    s_own, s_q, s_d, s_f, r_d, r_den, s_g, r_g, s_x, s_b, s_sq, r_sq, s_sib, s_c, r_c,
    r_q, r_p, r_m, r_p2, r_m2, r_cin, r_b,
):
    x = lax.axis_index("subj")
    f = lax.axis_index("fix")
    xp, xm, x2 = lax.rem(x + 1, NX), lax.rem(x + 3, NX), lax.rem(x + 2, NX)
    half = QUART // 2
    dpart = DIRECT // NDIR

    own_dens = pltpu.make_async_copy(dens_hbm, dens, s_own.at[0])
    own_dens.start()
    own_rows = pl.ds(f * PAIR, PAIR)
    own_weight = pltpu.make_async_copy(weight.at[own_rows], wbuf.at[own_rows], s_own.at[1])
    own_weight.start()

    barrier = pltpu.get_barrier_semaphore()

    def greet(k, carry):
        pl.semaphore_signal(barrier, inc=1, device_id=(x, lax.rem(f + k, NF)), device_id_type=MESH)
        return carry

    lax.fori_loop(1, NF, greet, 0)
    for t in (xp, xm, x2):
        pl.semaphore_signal(barrier, inc=1, device_id=(t, f), device_id_type=MESH)
    pl.semaphore_wait(barrier, NF - 1 + 3)

    def send_quarter(i, carry):
        t = ahead(f, offset(i))
        remote(
            weight.at[pl.ds(t * PAIR + x * QUART, QUART)],
            wbuf.at[pl.ds(f * PAIR + x * QUART, QUART)],
            s_q, r_q.at[i], (x, t),
        ).start()
        return carry

    lax.fori_loop(0, PEERS, send_quarter, 0)

    sib = f + 1 - 2 * lax.rem(f, 2)

    def to_sibling():
        return remote(
            weight.at[pl.ds(sib * PAIR, PAIR)], wbuf.at[pl.ds(f * PAIR, PAIR)], s_sib.at[0], s_sib.at[1], (x, sib)
        )

    to_sibling().start()

    cov_t = (design_t[...].astype(jnp.float32) - 7.5) * 0.25
    cov_wide = cov_t.T
    cov = cov_wide.astype(jnp.bfloat16)
    cov_half_t = cov_t.astype(jnp.bfloat16)
    for i in range(3):
        cov3[:, i * COV : (i + 1) * COV] = cov
    gbuf[x] = jnp.dot(cov_half_t, cov, preferred_element_type=jnp.float32)
    for t in (xp, xm, x2):
        remote(gbuf.at[x], gbuf.at[x], s_g, r_g, (t, f)).start()

    wbuf[SLOTS * PER :] = jnp.zeros((PER, UNIT, BLOCK), jnp.bfloat16)
    own_dens.wait()

    lane = lax.broadcasted_iota(jnp.int32, (8, BLOCK), 1)
    sub = lax.broadcasted_iota(jnp.int32, (8, BLOCK), 0)

    def gather_for(t):
        def own(c, carry):
            stage[t, c] = dens[t * FB + c]
            return carry

        def neighbour(h, carry):
            stage[t, FB + h] = dens[h * FB + nbr_ref[t, h]]
            return carry

        for c in range(FB):
            own(c, 0)
        for h in range(NF):
            neighbour(h, 0)
    spot = sub * BLOCK + lane

    def codes_for(t):
        codes = jnp.zeros((1, BLOCK), jnp.int32)
        for k in range(CAP):
            code = rows_ref[t * CAP + k] * SRC + cols_ref[t * CAP + k]
            codes = jnp.where(lane[:1] == k, code, codes)
        return codes

    def send_side(t):
        gather_for(t)
        cstage[t] = codes_for(t)
        remote(cstage.at[t], cbuf.at[f], s_c, r_c, (x, t)).start()
        remote(stage.at[t], den.at[f], s_d, r_den, (x, t)).start()

    def send_direct(i):
        t = ahead(f, offset(lax.rem(i, PEERS)))
        r = 4 * QUART + (i // PEERS) * dpart
        remote(
            weight.at[pl.ds(t * PAIR + r, dpart)],
            wbuf.at[pl.ds(f * PAIR + r, dpart)],
            s_d, r_d, (x, t),
        ).start()

    def pass_on(i):
        s = behind(f, offset(i))
        r = wbuf.at[pl.ds(s * PAIR + x * QUART, QUART)]
        remote(r, r, s_q, r_q.at[i], (x, f)).wait_recv()
        remote(r, r, s_f, r_p.at[i], (xp, f)).start()
        remote(r, r, s_f, r_m.at[i], (xm, f)).start()

    def pass_half(i):
        s = behind(f, offset(i))
        b = s * PAIR + xm * QUART
        r = wbuf.at[pl.ds(b, QUART)]
        remote(r, r, s_f, r_p.at[i], (xp, f)).wait_recv()
        r = wbuf.at[pl.ds(b, half)]
        remote(r, r, s_f, r_p2.at[i], (xp, f)).start()
        b = s * PAIR + xp * QUART
        r = wbuf.at[pl.ds(b, QUART)]
        remote(r, r, s_f, r_m.at[i], (xm, f)).wait_recv()
        r = wbuf.at[pl.ds(b + half, half)]
        remote(r, r, s_f, r_m2.at[i], (xm, f)).start()

    row_id = lax.broadcasted_iota(jnp.int32, (COV, 2 * COV), 0)
    lane_id = lax.broadcasted_iota(jnp.int32, (COV, 2 * COV), 1)

    def eliminate(j):
        m = mat[...]
        row = jnp.sum(jnp.where(row_id == j, m, 0.0), axis=0, keepdims=True)
        col = jnp.sum(jnp.where(lane_id == j, m, 0.0), axis=1, keepdims=True)
        pivot = jnp.sum(jnp.where((row_id == j) & (lane_id == j), m, 0.0), keepdims=True)
        factor = jnp.where(row_id > j, col / pivot, 0.0)
        mat[...] = m - factor * row

    eye = (
        lax.broadcasted_iota(jnp.int32, (COV, COV), 0) == lax.broadcasted_iota(jnp.int32, (COV, COV), 1)
    )

    def all_gram():
        return remote(gbuf.at[pl.ds(0, 3)], gbuf.at[pl.ds(0, 3)], s_g, r_g, (xp, f))

    def all_codes():
        return remote(cbuf.at[pl.ds(0, NF - 1)], cbuf.at[pl.ds(0, NF - 1)], s_c, r_c, (xp, f))

    def locate(s, acc):
        tile = cbuf[s]
        for k in range(CAP):
            acc = jnp.where(spot == tile[:, k : k + 1], s * CAP + k, acc)
        return acc

    def lay_out(c):
        block = den[:, c].astype(jnp.float32).reshape(ROWS, BLOCK)
        src[:, pl.ds(aligned(c * BLOCK, BLOCK), BLOCK)] = block.astype(jnp.bfloat16)

    def step(i, carry):
        @pl.when(i < PEERS)
        def _():
            pass_on(i)

        @pl.when(i >= LAG)
        def _():
            pass_half(i - LAG)

        @pl.when(i < PEERS // 2)
        def _():
            for e in range(2):
                send_side(ahead(f, offset(2 * i + e)))

        @pl.when((i >= PEERS // 2) & (i < PEERS))
        def _():
            for e in range(2 * NDIR):
                send_direct((i - PEERS // 2) * 2 * NDIR + e)

        @pl.when(i == ELIM_AT - 1)
        def _():
            all_gram().wait_recv()
            mat[:, :COV] = (gbuf[0] + gbuf[1]) + (gbuf[2] + gbuf[3])
            mat[:, COV:] = jnp.where(eye, 1.0, 0.0)

        @pl.when((i >= ELIM_AT) & (i < ELIM_AT + COV // 4))
        def _():
            for e in range(4):
                eliminate((i - ELIM_AT) * 4 + e)

        @pl.when(i == ELIM_AT + COV // 4)
        def _():
            diag = jnp.sum(jnp.where(eye, mat[:, :COV], 0.0), axis=1, keepdims=True)
            lower = mat[:, COV:] / jnp.sqrt(diag)
            lower_t = lower.T
            inverse = jnp.dot(lower_t, lower, preferred_element_type=jnp.float32, precision=lax.Precision.HIGHEST)
            g1, g2, g3 = three(inverse)
            solver[...] = jnp.concatenate([g1, g1, g1, g2, g2, g3], axis=1)
            invd[...] = lax.rsqrt(jnp.sum(lower_t * lower_t, axis=1, keepdims=True))

        @pl.when(i == LAY_AT - 1)
        def _():
            all_codes().wait_recv()
            idx_v[...] = lax.fori_loop(0, NF, locate, jnp.full((8, BLOCK), SLOTS, jnp.int32))
            to_smem = pltpu.make_async_copy(idx_v, idx_s, s_own.at[0])
            to_smem.start()
            to_smem.wait()

        @pl.when(i == LAY_AT - 1)
        def _():
            remote(den.at[pl.ds(0, NF - 1)], den.at[pl.ds(0, NF - 1)], s_d, r_den, (xp, f)).wait_recv()

        for e in range(LAY_STEP):
            c = (i - LAY_AT) * LAY_STEP + e

            @pl.when((c >= 0) & (c < SRC))
            def _():
                lay_out(c)

        return carry

    send_side(sib)
    gather_for(f)
    den[f] = stage[f]
    cbuf[f] = codes_for(f)
    lax.fori_loop(0, PEERS + LAG, step, 0)

    own_weight.wait()
    to_sibling().wait_recv()

    def last_halves(i, carry):
        r = wbuf.at[pl.ds(0, half)]
        remote(r, r, s_f, r_p2.at[i], (xp, f)).wait_recv()
        remote(r, r, s_f, r_m2.at[i], (xm, f)).wait_recv()
        return carry

    lax.fori_loop(0, PEERS, last_halves, 0)
    r = wbuf.at[pl.ds(0, PEERS * DIRECT)]
    remote(r, r, s_d, r_d, (xp, f)).wait_recv()

    def smooth_pair(n, halves):
        firsts = [group * 4 + h * 2 for group, h in halves]

        def block(first, c):
            p = first * SRC + c
            i = idx_s[p // BLOCK, lax.rem(p, BLOCK)]
            return jnp.concatenate([wbuf[i * PER + u] for u in range(PER)], axis=0)

        spread = None
        for c0 in range(0, SRC, KSTEP):
            right = jnp.concatenate(
                [
                    jnp.concatenate([block(first + e, c) for first in firsts for e in range(2)], axis=1)
                    for c in range(c0, c0 + KSTEP)
                ],
                axis=0,
            )
            part = jnp.dot(
                src[:, c0 * BLOCK : (c0 + KSTEP) * BLOCK], right, preferred_element_type=jnp.float32
            )
            spread = part if spread is None else spread + part
        for e, first in enumerate(firsts):
            at = pl.ds(aligned(first * BLOCK, BLOCK), CHUNK)
            own = src[:, at].astype(jnp.float32)
            part = (SELF_WEIGHT * own + spread[:, e * CHUNK : (e + 1) * CHUNK]).astype(jnp.bfloat16)
            smooth[:, at] = part
            cpart[2 * n + e] = jnp.dot(cov_half_t, part, preferred_element_type=jnp.float32)

    def send_part(n, rel, h, t):
        remote(cpart.at[n], cin.at[rel, h], s_x, r_cin.at[rel * 2 + h], (t, f)).start()

    smooth_pair(0, ((x2, 0), (x2, 1)))
    send_part(0, 0, 0, x2)
    send_part(1, 0, 1, x2)
    for h in range(2):
        smooth_pair(1 + h, ((xp, h), (xm, h)))
        send_part(2 + 2 * h, 1, h, xp)
        send_part(3 + 2 * h, 2, h, xm)
    smooth_pair(3, ((x, 0), (x, 1)))

    for h in range(2):
        total = cpart[NCHUNK - 2 + h]
        for rel in range(3):
            remote(cpart.at[0], cin.at[rel, h], s_x, r_cin.at[rel * 2 + h], (xp, f)).wait_recv()
            total = total + cin[rel, h]
        t1, t2, t3 = three(total)
        right = jnp.concatenate([t1, t2, t3, t1, t2, t1], axis=0)
        bbuf[x, :, h * CHUNK : (h + 1) * CHUNK] = jnp.dot(solver[...], right, preferred_element_type=jnp.float32)
    for rel, t in enumerate((xp, xm, x2)):
        remote(bbuf.at[x], bbuf.at[x], s_b, r_b.at[rel], (t, f)).start()

    def residual(group):
        at = pl.ds(aligned(group * GROUP, GROUP), GROUP)
        beta = bbuf[group]
        parts = jnp.concatenate(three(beta), axis=0)
        fitted = jnp.dot(cov3[...], parts, preferred_element_type=jnp.float32)
        res = smooth[:, at].astype(jnp.float32) - fitted
        resid[:, at] = res
        sqbuf[x, :, at] = jnp.sum(res * res, axis=0, keepdims=True)

    residual(x)
    for rel, t in enumerate((xm, xp, x2)):
        remote(bbuf.at[t], bbuf.at[t], s_b, r_b.at[rel], (t, f)).wait_recv()
        residual(t)
    for t in (xp, xm, x2):
        remote(sqbuf.at[x], sqbuf.at[x], s_sq, r_sq, (t, f)).start()
    for g in range(NX):
        coef[:, g * GROUP : (g + 1) * GROUP] = bbuf[g] * invd[...]
    whole = remote(sqbuf.at[pl.ds(0, 3)], sqbuf.at[pl.ds(0, 3)], s_sq, r_sq, (xp, f))
    whole.wait_recv()
    variance = ((sqbuf[0] + sqbuf[1]) + (sqbuf[2] + sqbuf[3])) / (ROWS * NX - COV)
    scaling[...] = lax.rsqrt(variance + EPSILON)

    r = wbuf.at[pl.ds(0, PEERS * QUART)]
    remote(r, r, s_q, r_d, (xp, f)).wait_send()
    r = wbuf.at[pl.ds(0, 3 * PEERS * QUART)]
    remote(r, r, s_f, r_d, (xp, f)).wait_send()
    r = wbuf.at[pl.ds(0, PEERS * DIRECT + (NF - 1) * SRC * 8 // UNIT)]
    remote(r, r, s_d, r_d, (xp, f)).wait_send()
    to_sibling().wait_send()
    all_gram().wait_send()
    all_codes().wait_send()
    r = cpart.at[pl.ds(0, NCHUNK - 2)]
    remote(r, r, s_x, r_d, (xp, f)).wait_send()
    r = bbuf.at[pl.ds(0, 3)]
    remote(r, r, s_b, r_d, (xp, f)).wait_send()
    whole.wait_send()


def scale(residual, coefficients, scaling, scores, effects, half_scores, half_effects, sems):
    by = scaling[...]
    part = ROWS // NX
    copies = [pltpu.make_async_copy(half_effects, effects, sems.at[NX])]
    half_effects[...] = coefficients[...] * by
    copies[0].start()
    for i in range(NX):
        rows = pl.ds(i * part, part)
        half_scores[i] = (residual[rows, :] * by).astype(jnp.bfloat16)
        copies.append(pltpu.make_async_copy(half_scores.at[i], scores.at[rows], sems.at[i]))
        copies[-1].start()
    for copy in copies:
        copy.wait()


def shards(density, conn_weight, conn_rows, conn_cols, nbr_list, design):
    dens = density.reshape(8, NF * FB, BLOCK).transpose(1, 0, 2)
    weight = conn_weight.reshape(NF * PAIR, UNIT, BLOCK)
    smem = pl.BlockSpec(memory_space=pltpu.SMEM)
    anywhere = pl.BlockSpec(memory_space=pl.ANY)
    vmem = pl.BlockSpec(memory_space=pltpu.VMEM)
    f32, bf16, i32 = jnp.float32, jnp.bfloat16, jnp.int32
    dma = pltpu.SemaphoreType.DMA
    residual, coefficients, scaling = pl.pallas_call(
        kernel,
        out_shape=(
            pltpu.VMEM((ROWS, COLS), f32),
            pltpu.VMEM((COV, COLS), f32),
            pltpu.VMEM((1, COLS), f32),
        ),
        in_specs=[smem, smem, smem, anywhere, anywhere, vmem],
        out_specs=(vmem, vmem, vmem),
        scratch_shapes=[
            pltpu.VMEM((NF * FB, 8, BLOCK), bf16),
            pltpu.VMEM(((SLOTS + 1) * PER, UNIT, BLOCK), bf16),
            pltpu.VMEM((NF, SRC, 8, BLOCK), bf16),
            pltpu.VMEM((NF, SRC, 8, BLOCK), bf16),
            pltpu.VMEM((ROWS, SRC * BLOCK), bf16),
            pltpu.VMEM((NF, 1, BLOCK), i32),
            pltpu.VMEM((NF, 1, BLOCK), i32),
            pltpu.VMEM((8, BLOCK), i32),
            pltpu.SMEM((8, BLOCK), i32),
            pltpu.VMEM((NX, COV, COV), f32),
            pltpu.VMEM((COV, 2 * COV), f32),
            pltpu.VMEM((COV, 6 * COV), bf16),
            pltpu.VMEM((COV, 1), f32),
            pltpu.VMEM((ROWS, COLS), bf16),
            pltpu.VMEM((ROWS, 3 * COV), bf16),
            pltpu.VMEM((NCHUNK, COV, CHUNK), f32),
            pltpu.VMEM((3, 2, COV, CHUNK), f32),
            pltpu.VMEM((NX, COV, GROUP), f32),
            pltpu.VMEM((NX, 1, COLS), f32),
            dma((2,)),
        ]
        + [dma] * 11
        + [dma((2,)), dma, dma]
        + [dma((PEERS,))] * 5
        + [dma((NCHUNK - 2,)), dma((3,))],
        compiler_params=pltpu.CompilerParams(
            collective_id=0, has_side_effects=True, vmem_limit_bytes=56 * 2**20
        ),
        cost_estimate=pl.CostEstimate(flops=2 * ROWS * SRC * BLOCK * COLS, bytes_accessed=30 << 20, transcendentals=0),
    )(conn_rows, conn_cols, nbr_list.reshape(NF, NF), dens, weight, design.T)

    return pl.pallas_call(
        scale,
        out_shape=(jax.ShapeDtypeStruct((ROWS, COLS), bf16), jax.ShapeDtypeStruct((COV, COLS), f32)),
        in_specs=[vmem, vmem, vmem],
        out_specs=(anywhere, anywhere),
        scratch_shapes=[pltpu.VMEM((NX, ROWS // NX, COLS), bf16), pltpu.VMEM((COV, COLS), f32), dma((NX + 1,))],
        compiler_params=pltpu.CompilerParams(vmem_limit_bytes=16 * 2**20),
    )(residual, coefficients, scaling)


def solution(mesh):
    in_specs = (
        P(("subj", "fix"), None),
        P("fix", None, None),
        P("fix"),
        P("fix"),
        P(),
        P("subj", None),
    )
    out_specs = (P("subj", "fix"), P(None, "fix"))
    return jax.shard_map(shards, mesh=mesh, in_specs=in_specs, out_specs=out_specs, check_vma=False)
```

```python
import functools
import jax
import jax.numpy as jnp
from jax import lax
from jax.experimental import pallas as pl
from jax.experimental.pallas import tpu as pltpu
from jax.sharding import PartitionSpec as P

MESH = pl.DeviceIdType.MESH
SELF_WEIGHT = 4.0
EPSILON = 1e-06

NX, NF = 4, 32
BLOCK = 128
FB = 16
SRC = 48
CAP = 12
UNIT = 32
PER = BLOCK // UNIT
COV = 64
PEERS = NF - 2
PAIR = CAP * PER
QUART = 10
DIRECT = PAIR - 4 * QUART
NDIR = 2
LAG = 4
ELIM_AT = 4
LAY_AT = 28
LAY_STEP = 8
KSTEP = 8
SLOTS = NF * CAP
COLS = FB * BLOCK
ROWS = 256
CHUNK = 2 * BLOCK
NCHUNK = COLS // CHUNK
GROUP = COLS // NX

_RING = ("01", "03", "10", "30", "11", "33", "13", "31", "20", "02", "12", "32", "21", "23", "22")
ORDER = [int(g[0]) * 8 + int(g[1]) * 2 + (c ^ (i & 1)) for c in (0, 1) for i, g in enumerate(_RING)]


def offset(k):
    words = [sum(v << (5 * i) for i, v in enumerate(ORDER[b : b + 6])) for b in range(0, PEERS, 6)]
    word = jnp.int32(words[0])
    for i in range(1, len(words)):
        word = jnp.where(k >= 6 * i, jnp.int32(words[i]), word)
    return (word >> (5 * lax.rem(k, 6))) & 31


def split(f):
    return f // 8, (f // 2) % 4, f % 2


def ahead(f, o):
    z, y, c = split(f)
    a, b, d = split(o)
    turn = 1 - 2 * c
    return lax.rem(z + 4 + turn * a, 4) * 8 + lax.rem(y + 4 + turn * b, 4) * 2 + lax.rem(c + d, 2)


def behind(f, o):
    z, y, c = split(f)
    a, b, d = split(o)
    sender = lax.rem(c + d, 2)
    turn = 1 - 2 * sender
    return lax.rem(z + 4 - turn * a, 4) * 8 + lax.rem(y + 4 - turn * b, 4) * 2 + sender


def remote(src, dst, send, recv, device):
    return pltpu.make_async_remote_copy(src, dst, send, recv, device_id=device, device_id_type=MESH)


def three(v):
    a = v.astype(jnp.bfloat16)
    v = v - a.astype(jnp.float32)
    b = v.astype(jnp.bfloat16)
    return a, b, (v - b.astype(jnp.float32)).astype(jnp.bfloat16)


def aligned(v, n):
    return pl.multiple_of(v, n)


def kernel(
    rows_ref, cols_ref, nbr_ref, dens_hbm, weight, design_t,
    resid, coef, scaling,
    dens, wbuf, stage, den, src, cstage, cbuf, idx_v, idx_s, gbuf, mat, solver, invd,
    smooth, cov3, cpart, cin, bbuf, sqbuf,
    s_own, s_q, s_d, s_f, r_d, r_den, s_g, r_g, s_x, s_b, s_sq, r_sq, s_sib, s_c, r_c,
    r_q, r_p, r_m, r_p2, r_m2, r_cin, r_b,
):
    x = lax.axis_index("subj")
    f = lax.axis_index("fix")
    xp, xm, x2 = lax.rem(x + 1, NX), lax.rem(x + 3, NX), lax.rem(x + 2, NX)
    half = QUART // 2
    dpart = DIRECT // NDIR

    own_dens = pltpu.make_async_copy(dens_hbm, dens, s_own.at[0])
    own_dens.start()
    own_rows = pl.ds(f * PAIR, PAIR)
    own_weight = pltpu.make_async_copy(weight.at[own_rows], wbuf.at[own_rows], s_own.at[1])
    own_weight.start()

    barrier = pltpu.get_barrier_semaphore()

    def greet(k, carry):
        pl.semaphore_signal(barrier, inc=1, device_id=(x, lax.rem(f + k, NF)), device_id_type=MESH)
        return carry

    lax.fori_loop(1, NF, greet, 0)
    for t in (xp, xm, x2):
        pl.semaphore_signal(barrier, inc=1, device_id=(t, f), device_id_type=MESH)
    pl.semaphore_wait(barrier, NF - 1 + 3)

    def send_quarter(i, carry):
        t = ahead(f, offset(i))
        remote(
            weight.at[pl.ds(t * PAIR + x * QUART, QUART)],
            wbuf.at[pl.ds(f * PAIR + x * QUART, QUART)],
            s_q, r_q.at[i], (x, t),
        ).start()
        return carry

    lax.fori_loop(0, PEERS, send_quarter, 0)

    sib = f + 1 - 2 * lax.rem(f, 2)

    def to_sibling():
        return remote(
            weight.at[pl.ds(sib * PAIR, PAIR)], wbuf.at[pl.ds(f * PAIR, PAIR)], s_sib.at[0], s_sib.at[1], (x, sib)
        )

    to_sibling().start()

    cov_t = (design_t[...].astype(jnp.float32) - 7.5) * 0.25
    cov_wide = cov_t.T
    cov = cov_wide.astype(jnp.bfloat16)
    cov_half_t = cov_t.astype(jnp.bfloat16)
    for i in range(3):
        cov3[:, i * COV : (i + 1) * COV] = cov
    gbuf[x] = jnp.dot(cov_half_t, cov, preferred_element_type=jnp.float32)
    for t in (xp, xm, x2):
        remote(gbuf.at[x], gbuf.at[x], s_g, r_g, (t, f)).start()

    wbuf[SLOTS * PER :] = jnp.zeros((PER, UNIT, BLOCK), jnp.bfloat16)
    own_dens.wait()

    lane = lax.broadcasted_iota(jnp.int32, (8, BLOCK), 1)
    sub = lax.broadcasted_iota(jnp.int32, (8, BLOCK), 0)

    def gather_for(t):
        def own(c, carry):
            stage[t, c] = dens[t * FB + c]
            return carry

        def neighbour(h, carry):
            stage[t, FB + h] = dens[h * FB + nbr_ref[t, h]]
            return carry

        for c in range(FB):
            own(c, 0)
        for h in range(NF):
            neighbour(h, 0)
    spot = sub * BLOCK + lane

    def codes_for(t):
        codes = jnp.zeros((1, BLOCK), jnp.int32)
        for k in range(CAP):
            code = rows_ref[t * CAP + k] * SRC + cols_ref[t * CAP + k]
            codes = jnp.where(lane[:1] == k, code, codes)
        return codes

    def send_side(t):
        gather_for(t)
        cstage[t] = codes_for(t)
        remote(cstage.at[t], cbuf.at[f], s_c, r_c, (x, t)).start()
        remote(stage.at[t], den.at[f], s_d, r_den, (x, t)).start()

    def send_direct(i):
        t = ahead(f, offset(lax.rem(i, PEERS)))
        r = 4 * QUART + (i // PEERS) * dpart
        remote(
            weight.at[pl.ds(t * PAIR + r, dpart)],
            wbuf.at[pl.ds(f * PAIR + r, dpart)],
            s_d, r_d, (x, t),
        ).start()

    def pass_on(i):
        s = behind(f, offset(i))
        r = wbuf.at[pl.ds(s * PAIR + x * QUART, QUART)]
        remote(r, r, s_q, r_q.at[i], (x, f)).wait_recv()
        remote(r, r, s_f, r_p.at[i], (xp, f)).start()
        remote(r, r, s_f, r_m.at[i], (xm, f)).start()

    def pass_half(i):
        s = behind(f, offset(i))
        b = s * PAIR + xm * QUART
        r = wbuf.at[pl.ds(b, QUART)]
        remote(r, r, s_f, r_p.at[i], (xp, f)).wait_recv()
        r = wbuf.at[pl.ds(b, half)]
        remote(r, r, s_f, r_p2.at[i], (xp, f)).start()
        b = s * PAIR + xp * QUART
        r = wbuf.at[pl.ds(b, QUART)]
        remote(r, r, s_f, r_m.at[i], (xm, f)).wait_recv()
        r = wbuf.at[pl.ds(b + half, half)]
        remote(r, r, s_f, r_m2.at[i], (xm, f)).start()

    row_id = lax.broadcasted_iota(jnp.int32, (COV, 2 * COV), 0)
    lane_id = lax.broadcasted_iota(jnp.int32, (COV, 2 * COV), 1)

    def eliminate(j):
        m = mat[...]
        row = jnp.sum(jnp.where(row_id == j, m, 0.0), axis=0, keepdims=True)
        col = jnp.sum(jnp.where(lane_id == j, m, 0.0), axis=1, keepdims=True)
        pivot = jnp.sum(jnp.where((row_id == j) & (lane_id == j), m, 0.0), keepdims=True)
        factor = jnp.where(row_id > j, col / pivot, 0.0)
        mat[...] = m - factor * row

    eye = (
        lax.broadcasted_iota(jnp.int32, (COV, COV), 0) == lax.broadcasted_iota(jnp.int32, (COV, COV), 1)
    )

    def all_gram():
        return remote(gbuf.at[pl.ds(0, 3)], gbuf.at[pl.ds(0, 3)], s_g, r_g, (xp, f))

    def all_codes():
        return remote(cbuf.at[pl.ds(0, NF - 1)], cbuf.at[pl.ds(0, NF - 1)], s_c, r_c, (xp, f))

    def locate(s, acc):
        tile = cbuf[s]
        for k in range(CAP):
            acc = jnp.where(spot == tile[:, k : k + 1], s * CAP + k, acc)
        return acc

    def lay_out(c):
        block = den[:, c].astype(jnp.float32).reshape(ROWS, BLOCK)
        src[:, pl.ds(aligned(c * BLOCK, BLOCK), BLOCK)] = block.astype(jnp.bfloat16)

    def step(i, carry):
        @pl.when(i < PEERS)
        def _():
            pass_on(i)

        @pl.when(i >= LAG)
        def _():
            pass_half(i - LAG)

        @pl.when(i < PEERS // 2)
        def _():
            for e in range(2):
                send_side(ahead(f, offset(2 * i + e)))

        @pl.when((i >= PEERS // 2) & (i < PEERS))
        def _():
            for e in range(2 * NDIR):
                send_direct((i - PEERS // 2) * 2 * NDIR + e)

        @pl.when(i == ELIM_AT - 1)
        def _():
            all_gram().wait_recv()
            mat[:, :COV] = (gbuf[0] + gbuf[1]) + (gbuf[2] + gbuf[3])
            mat[:, COV:] = jnp.where(eye, 1.0, 0.0)

        @pl.when((i >= ELIM_AT) & (i < ELIM_AT + COV // 4))
        def _():
            for e in range(4):
                eliminate((i - ELIM_AT) * 4 + e)

        @pl.when(i == ELIM_AT + COV // 4)
        def _():
            diag = jnp.sum(jnp.where(eye, mat[:, :COV], 0.0), axis=1, keepdims=True)
            lower = mat[:, COV:] / jnp.sqrt(diag)
            lower_t = lower.T
            inverse = jnp.dot(lower_t, lower, preferred_element_type=jnp.float32, precision=lax.Precision.HIGHEST)
            g1, g2, g3 = three(inverse)
            solver[...] = jnp.concatenate([g1, g1, g1, g2, g2, g3], axis=1)
            invd[...] = lax.rsqrt(jnp.sum(lower_t * lower_t, axis=1, keepdims=True))

        @pl.when(i == LAY_AT - 1)
        def _():
            all_codes().wait_recv()
            idx_v[...] = lax.fori_loop(0, NF, locate, jnp.full((8, BLOCK), SLOTS, jnp.int32))
            to_smem = pltpu.make_async_copy(idx_v, idx_s, s_own.at[0])
            to_smem.start()
            to_smem.wait()

        @pl.when(i == LAY_AT - 1)
        def _():
            remote(den.at[pl.ds(0, NF - 1)], den.at[pl.ds(0, NF - 1)], s_d, r_den, (xp, f)).wait_recv()

        for e in range(LAY_STEP):
            c = (i - LAY_AT) * LAY_STEP + e

            @pl.when((c >= 0) & (c < SRC))
            def _():
                lay_out(c)

        return carry

    send_side(sib)
    gather_for(f)
    den[f] = stage[f]
    cbuf[f] = codes_for(f)
    lax.fori_loop(0, PEERS + LAG, step, 0)

    own_weight.wait()
    to_sibling().wait_recv()

    def last_halves(i, carry):
        r = wbuf.at[pl.ds(0, half)]
        remote(r, r, s_f, r_p2.at[i], (xp, f)).wait_recv()
        remote(r, r, s_f, r_m2.at[i], (xm, f)).wait_recv()
        return carry

    lax.fori_loop(0, PEERS, last_halves, 0)
    r = wbuf.at[pl.ds(0, PEERS * DIRECT)]
    remote(r, r, s_d, r_d, (xp, f)).wait_recv()

    def smooth_pair(n, halves):
        firsts = [group * 4 + h * 2 for group, h in halves]

        def block(first, c):
            p = first * SRC + c
            i = idx_s[p // BLOCK, lax.rem(p, BLOCK)]
            return jnp.concatenate([wbuf[i * PER + u] for u in range(PER)], axis=0)

        spread = None
        for c0 in range(0, SRC, KSTEP):
            right = jnp.concatenate(
                [
                    jnp.concatenate([block(first + e, c) for first in firsts for e in range(2)], axis=1)
                    for c in range(c0, c0 + KSTEP)
                ],
                axis=0,
            )
            part = jnp.dot(
                src[:, c0 * BLOCK : (c0 + KSTEP) * BLOCK], right, preferred_element_type=jnp.float32
            )
            spread = part if spread is None else spread + part
        for e, first in enumerate(firsts):
            at = pl.ds(aligned(first * BLOCK, BLOCK), CHUNK)
            own = src[:, at].astype(jnp.float32)
            part = (SELF_WEIGHT * own + spread[:, e * CHUNK : (e + 1) * CHUNK]).astype(jnp.bfloat16)
            smooth[:, at] = part
            cpart[n + e] = jnp.dot(cov_half_t, part, preferred_element_type=jnp.float32)

    def send_part(n, rel, h, t):
        remote(cpart.at[n], cin.at[rel, h], s_x, r_cin.at[rel * 2 + h], (t, f)).start()

    def half_beta(slot, h, rel, t):
        return remote(bbuf.at[slot, h], bbuf.at[slot, h], s_b, r_b.at[2 * rel + h], (t, f))

    def solve(h):
        total = cpart[4 * h + 3]
        for rel in range(3):
            remote(cpart.at[0], cin.at[rel, h], s_x, r_cin.at[rel * 2 + h], (xp, f)).wait_recv()
            total = total + cin[rel, h]
        t1, t2, t3 = three(total)
        right = jnp.concatenate([t1, t2, t3, t1, t2, t1], axis=0)
        bbuf[x, h] = jnp.dot(solver[...], right, preferred_element_type=jnp.float32)
        half_beta(x, h, 2, x2).start()
        half_beta(x, h, 0, xp).start()
        half_beta(x, h, 1, xm).start()

    smooth_pair(0, ((x2, 0), (xp, 0)))
    send_part(0, 0, 0, x2)
    send_part(1, 1, 0, xp)
    smooth_pair(2, ((xm, 0), (x, 0)))
    send_part(2, 2, 0, xm)
    smooth_pair(4, ((x2, 1), (xp, 1)))
    send_part(4, 0, 1, x2)
    send_part(5, 1, 1, xp)
    smooth_pair(6, ((xm, 1),))
    send_part(6, 2, 1, xm)
    solve(0)
    smooth_pair(7, ((x, 1),))
    solve(1)

    def residual(group, h):
        at = pl.ds(aligned(group * GROUP + h * CHUNK, CHUNK), CHUNK)
        parts = jnp.concatenate(three(bbuf[group, h]), axis=0)
        fitted = jnp.dot(cov3[...], parts, preferred_element_type=jnp.float32)
        res = smooth[:, at].astype(jnp.float32) - fitted
        resid[:, at] = res
        sqbuf[x, :, at] = jnp.sum(res * res, axis=0, keepdims=True)

    for h in range(2):
        residual(x, h)
        for rel, t in enumerate((xm, xp, x2)):
            half_beta(t, h, rel, t).wait_recv()
            residual(t, h)
    for t in (xp, xm, x2):
        remote(sqbuf.at[x], sqbuf.at[x], s_sq, r_sq, (t, f)).start()
    for g in range(NX):
        for h in range(2):
            coef[:, g * GROUP + h * CHUNK : g * GROUP + (h + 1) * CHUNK] = bbuf[g, h] * invd[...]
    whole = remote(sqbuf.at[pl.ds(0, 3)], sqbuf.at[pl.ds(0, 3)], s_sq, r_sq, (xp, f))
    r = wbuf.at[pl.ds(0, PEERS * QUART)]
    remote(r, r, s_q, r_d, (xp, f)).wait_send()
    r = wbuf.at[pl.ds(0, 3 * PEERS * QUART)]
    remote(r, r, s_f, r_d, (xp, f)).wait_send()
    r = wbuf.at[pl.ds(0, PEERS * DIRECT + (NF - 1) * SRC * 8 // UNIT)]
    remote(r, r, s_d, r_d, (xp, f)).wait_send()
    to_sibling().wait_send()
    all_gram().wait_send()
    all_codes().wait_send()
    r = cpart.at[pl.ds(0, NCHUNK - 2)]
    remote(r, r, s_x, r_d, (xp, f)).wait_send()
    r = bbuf.at[pl.ds(0, 3)]
    remote(r, r, s_b, r_d, (xp, f)).wait_send()
    whole.wait_recv()
    variance = ((sqbuf[0] + sqbuf[1]) + (sqbuf[2] + sqbuf[3])) / (ROWS * NX - COV)
    scaling[...] = lax.rsqrt(variance + EPSILON)

    whole.wait_send()


def scale(residual, coefficients, scaling, scores, effects, half_scores, half_effects, sems):
    by = scaling[...]
    part = ROWS // NX
    copies = [pltpu.make_async_copy(half_effects, effects, sems.at[NX])]
    half_effects[...] = coefficients[...] * by
    copies[0].start()
    for i in range(NX):
        rows = pl.ds(i * part, part)
        half_scores[i] = (residual[rows, :] * by).astype(jnp.bfloat16)
        copies.append(pltpu.make_async_copy(half_scores.at[i], scores.at[rows], sems.at[i]))
        copies[-1].start()
    for copy in copies:
        copy.wait()


def shards(density, conn_weight, conn_rows, conn_cols, nbr_list, design):
    dens = density.reshape(8, NF * FB, BLOCK).transpose(1, 0, 2)
    weight = conn_weight.reshape(NF * PAIR, UNIT, BLOCK)
    smem = pl.BlockSpec(memory_space=pltpu.SMEM)
    anywhere = pl.BlockSpec(memory_space=pl.ANY)
    vmem = pl.BlockSpec(memory_space=pltpu.VMEM)
    f32, bf16, i32 = jnp.float32, jnp.bfloat16, jnp.int32
    dma = pltpu.SemaphoreType.DMA
    residual, coefficients, scaling = pl.pallas_call(
        kernel,
        out_shape=(
            pltpu.VMEM((ROWS, COLS), f32),
            pltpu.VMEM((COV, COLS), f32),
            pltpu.VMEM((1, COLS), f32),
        ),
        in_specs=[smem, smem, smem, anywhere, anywhere, vmem],
        out_specs=(vmem, vmem, vmem),
        scratch_shapes=[
            pltpu.VMEM((NF * FB, 8, BLOCK), bf16),
            pltpu.VMEM(((SLOTS + 1) * PER, UNIT, BLOCK), bf16),
            pltpu.VMEM((NF, SRC, 8, BLOCK), bf16),
            pltpu.VMEM((NF, SRC, 8, BLOCK), bf16),
            pltpu.VMEM((ROWS, SRC * BLOCK), bf16),
            pltpu.VMEM((NF, 1, BLOCK), i32),
            pltpu.VMEM((NF, 1, BLOCK), i32),
            pltpu.VMEM((8, BLOCK), i32),
            pltpu.SMEM((8, BLOCK), i32),
            pltpu.VMEM((NX, COV, COV), f32),
            pltpu.VMEM((COV, 2 * COV), f32),
            pltpu.VMEM((COV, 6 * COV), bf16),
            pltpu.VMEM((COV, 1), f32),
            pltpu.VMEM((ROWS, COLS), bf16),
            pltpu.VMEM((ROWS, 3 * COV), bf16),
            pltpu.VMEM((NCHUNK, COV, CHUNK), f32),
            pltpu.VMEM((3, 2, COV, CHUNK), f32),
            pltpu.VMEM((NX, 2, COV, CHUNK), f32),
            pltpu.VMEM((NX, 1, COLS), f32),
            dma((2,)),
        ]
        + [dma] * 11
        + [dma((2,)), dma, dma]
        + [dma((PEERS,))] * 5
        + [dma((NCHUNK - 2,)), dma((6,))],
        compiler_params=pltpu.CompilerParams(
            collective_id=0, has_side_effects=True, vmem_limit_bytes=56 * 2**20
        ),
        cost_estimate=pl.CostEstimate(flops=2 * ROWS * SRC * BLOCK * COLS, bytes_accessed=30 << 20, transcendentals=0),
    )(conn_rows, conn_cols, nbr_list.reshape(NF, NF), dens, weight, design.T)

    return pl.pallas_call(
        scale,
        out_shape=(jax.ShapeDtypeStruct((ROWS, COLS), bf16), jax.ShapeDtypeStruct((COV, COLS), f32)),
        in_specs=[vmem, vmem, vmem],
        out_specs=(anywhere, anywhere),
        scratch_shapes=[pltpu.VMEM((NX, ROWS // NX, COLS), bf16), pltpu.VMEM((COV, COLS), f32), dma((NX + 1,))],
        compiler_params=pltpu.CompilerParams(vmem_limit_bytes=16 * 2**20),
    )(residual, coefficients, scaling)


def solution(mesh):
    in_specs = (
        P(("subj", "fix"), None),
        P("fix", None, None),
        P("fix"),
        P("fix"),
        P(),
        P("subj", None),
    )
    out_specs = (P("subj", "fix"), P(None, "fix"))
    return jax.shard_map(shards, mesh=mesh, in_specs=in_specs, out_specs=out_specs, check_vma=False)
```
